1024 devices in a mesh: group: 4 (over x), ingroup: 32 (over z, core), cuts: 8 (over y).
Axes of the slice: x: 4, y: 8, z: 16, core: 2. Of those that a mesh axis runs over, the one named last changes fastest.
Arguments:
- tokens_q: bfloat16 [4096, 4096], P(('group', 'ingroup'), 'cuts'), may hold values from -6 to 6
- scale_exp: int32 [4096, 32], P(('group', 'ingroup'), 'cuts'), may hold values from -2 to 2
- routes: int32 [4096, 8], P(('group', 'ingroup')), may hold values from 0 to 127, all different within a row; in each aligned block of 32 rows (0 to 31, 32 to 63, ...) at most 4 rows name the same one
- route_scores: float32 [4096, 8], P(('group', 'ingroup')), may hold values from 0.05 to 1
- w_gate: bfloat16 [128, 4096, 1024], P(('group', 'ingroup'), 'cuts'), may hold values from -0.09375 to 0.09375
- w_up: bfloat16 [128, 4096, 1024], P(('group', 'ingroup'), 'cuts'), may hold values from -0.09375 to 0.09375
- w_down: bfloat16 [128, 1024, 4096], P(('group', 'ingroup'), None, 'cuts'), may hold values from -0.1875 to 0.1875
Outputs:
- mixed: bfloat16 [4096, 4096], P(('group', 'ingroup'), 'cuts')
The draws below stay inside these ranges and needn't reach their ends.
Inputs may be any that keep to these rules, and one draw needn't show every extreme that they name: `routes`: each row names 8 different experts. In each aligned block of 32 rows (the rows of one index of group and ingroup) no expert is named by more than 4 rows, and in some block an expert is named by exactly 4.
All inputs are finite; a program needn't handle non-finite values.
Results may differ from the reference program's by a relative error of at most 0.029.
Values may be sent and summed in bfloat16 or wider, within the bound.
No kernel may reach another device: no remote copies, remote signals or barrier semaphores. Data moves between devices by JAX's collectives and lax.ppermute only.
A program may use at most 32 MiB of HBM per device.

```python
import math
import jax
import jax.numpy as jnp
import numpy as np
from jax import lax

D = 4096
EH = 1024
TOPK = 8
TOK_DEV = 32
EXPERTS = 128
TOKENS = 4096
CAP = 4
N_CUTS = 8


def place_ends(result, stream_key, least, top_value):
    dims = result.shape
    spot = [jax.random.randint(jax.random.fold_in(stream_key, axis), (), 0, dims[axis]) for axis in range(len(dims))]
    result = result.at[tuple(spot)].set(least)
    longest = dims.index(max(dims))
    spot[longest] = (spot[longest] + 1) % dims[longest]
    return result.at[tuple(spot)].set(top_value)


def steps_of(rng, extent, cuts, least, high):
    def one(axis_at, shards_of):
        steps = jax.random.uniform(jax.random.fold_in(jax.random.fold_in(rng, 6), axis_at), (shards_of,), jnp.float32, least / len(cuts), high / len(cuts))
        return jnp.repeat(jnp.exp(steps), extent[axis_at] // shards_of).reshape((-1,) + (1,) * (len(extent) - axis_at - 1))

    loudness = one(*cuts[0])
    for cut in cuts[1:]:
        loudness = loudness * one(*cut)
    return loudness


def shared_out(rng, own, number, rows, number_of, top, most, slope):
    sequence = jax.random.permutation(rng, number_of)
    crowded, ordinary = load_shares(number_of, rows * top, most, slope, True), load_shares(number_of, rows * top, most, slope, False)
    places = jnp.arange(number_of)

    def named(sizes, rotation):
        used = int((sizes > 0).sum())
        fixed = max(1, used // 4)
        shifted = fixed + (places - fixed + rotation * (used - fixed)) % max(1, number_of - fixed)
        return jnp.zeros((number_of,), jnp.int32).at[sequence[jnp.where(places < fixed, places, shifted)]].set(jnp.asarray(sizes, jnp.int32))

    sizes = jnp.where(number % 4 == 0, named(crowded, number // 4), named(ordinary, number - number // 4 - 1))
    mixed = jax.random.permutation(jax.random.fold_in(own, 3), number_of)
    donor, receiver = mixed[0:number_of // 2 * 2:2], mixed[1:number_of // 2 * 2:2]
    slack = jnp.minimum(sizes[donor] - 1, most - sizes[receiver]) // 2
    slack = jnp.where((donor == sequence[0]) | (receiver == sequence[0]) | (sizes[receiver] == 0), 0, jnp.maximum(slack, 0))
    shifted = jax.random.randint(jax.random.fold_in(own, 4), (number_of // 2,), 0, 1 << 20) % (slack + 1)
    sizes = sizes.at[donor].add(-shifted).at[receiver].add(shifted)
    items = jnp.searchsorted(jnp.cumsum(sizes), jnp.arange(rows * top), side="right").astype(jnp.int32)
    listing = items.reshape(top, rows).T
    listing = listing[jax.random.permutation(jax.random.fold_in(own, 1), rows)]
    rotation = jax.random.randint(jax.random.fold_in(own, 2), (rows, 1), 0, top)
    return jnp.take_along_axis(listing, (jnp.arange(top)[None, :] + rotation) % top, axis=1)


def load_shares(count, total, reach, lean, full):
    weights = [(1 << 20) // math.isqrt(rank ** lean) + 1 for rank in range(1, count + 1)]
    largest = reach if full else min(reach, max(-(-total // count), total * weights[0] // sum(weights)))
    least = 1 if total - largest >= count - 1 else 0
    given, spare = [largest] + [least] * (count - 1), total - largest - least * (count - 1)
    while spare > 0:
        free = [i for i in range(1, count) if given[i] < largest] or [i for i in range(1, count) if given[i] < reach]
        whole, remaining = sum([weights[i] for i in free]), spare
        for i in free:
            addition = min(reach - given[i], max(1, remaining * weights[i] // whole), spare)
            given[i] = given[i] + addition
            spare = spare - addition
    return np.array(given)


def bell_draw(rng, dims, spread, most, cuts=(), kind=jnp.bfloat16):
    loudness = steps_of(rng, dims, cuts, -0.22, 0.18) if cuts else 1.0
    result = jax.random.normal(rng, dims, jnp.float32) * spread * loudness
    return jnp.minimum(jnp.maximum(result, -most), most).astype(kind)


def setup_inputs(seed: int = 0) -> dict:
    keys = jax.random.split(jax.random.key(seed), 8)
    tokens_q = bell_draw(keys[0], (TOKENS, D), 1.0, 6.0, ((0, 128), (1, 8)))
    scale_exp = place_ends(jax.random.randint(keys[1], (TOKENS, D // 128), -2, 3), jax.random.fold_in(keys[1], 1), -2, 2).astype(jnp.int32)
    routes_keys = jax.random.split(jax.random.fold_in(keys[2], 1), TOKENS // TOK_DEV)
    routes_turns = jax.random.permutation(jax.random.fold_in(keys[2], 3), TOKENS // TOK_DEV)
    routes = jax.vmap(lambda own, number: shared_out(jax.random.fold_in(keys[2], 2), own, number, TOK_DEV, EXPERTS, TOPK, CAP, 2))(routes_keys, routes_turns).reshape((TOKENS, TOPK))
    route_scores = jnp.clip(jnp.exp(math.log(1.0) - 2.9957323 * jax.random.uniform(keys[3], (TOKENS, TOPK), jnp.float32) ** steps_of(keys[3], (TOKENS, TOPK), ((0, 128),), -0.2, 0.2)), 0.05, 1.0)
    w_gate = bell_draw(keys[4], (EXPERTS, D, EH), D ** -0.5, 0.09375, ((0, 128), (1, 8)))
    w_up = bell_draw(keys[5], (EXPERTS, D, EH), D ** -0.5, 0.09375, ((0, 128), (1, 8)))
    w_down = bell_draw(keys[6], (EXPERTS, EH, D), EH ** -0.5, 0.1875, ((0, 128), (2, 8)))
    return dict(tokens_q=tokens_q, scale_exp=scale_exp, routes=routes, route_scores=route_scores, w_gate=w_gate, w_up=w_up, w_down=w_down)


def bf16_blocks(rows, weight):
    width = D // N_CUTS
    total = jnp.zeros((rows.shape[0], weight.shape[1]), jnp.float32)
    for piece_idx in range(N_CUTS):
        part = jnp.dot(rows[:, piece_idx * width:(piece_idx + 1) * width], weight[piece_idx * width:(piece_idx + 1) * width], preferred_element_type=jnp.float32)
        rounded = lax.optimization_barrier(part.astype(jnp.bfloat16))
        total = total + rounded.astype(jnp.float32)
    return total


def reference(tokens_q, scale_exp, routes, route_scores, w_gate, w_up, w_down):
    sources = TOKENS // TOK_DEV
    blocks = tokens_q.astype(jnp.float32).reshape(TOKENS, D // 128, 128)
    factor = jnp.exp2(scale_exp.astype(jnp.float32))[:, :, None]
    rows = (blocks * factor).reshape(TOKENS, D).astype(jnp.bfloat16)
    mix = (2.5 * route_scores / jnp.sum(route_scores, axis=1, keepdims=True)).astype(jnp.bfloat16)
    token_ids = jnp.arange(TOKENS, dtype=jnp.int32)
    named = jnp.zeros((TOKENS, EXPERTS), jnp.int32).at[token_ids[:, None], routes].add(1)
    named_blocks = named.reshape(sources, TOK_DEV, EXPERTS)
    before = (jnp.cumsum(named_blocks, axis=1, dtype=jnp.int32) - named_blocks).reshape(TOKENS, EXPERTS)
    route_slot = jnp.take_along_axis(before, routes, axis=1).astype(jnp.int32)
    position = ((token_ids // TOK_DEV)[:, None] * CAP + route_slot).astype(jnp.int32)
    table = jnp.full((EXPERTS, sources * CAP), TOKENS, jnp.int32)
    table = table.at[routes, position].set(jnp.broadcast_to(token_ids[:, None], (TOKENS, TOPK)))
    weights = jnp.zeros((EXPERTS, sources * CAP), jnp.float32).at[routes, position].set(mix.astype(jnp.float32))
    padded = jnp.concatenate([rows, jnp.zeros((1, D), jnp.bfloat16)], axis=0)

    def one_expert(total, inputs):
        index, weight, gate_w, up_w, down_w = inputs
        picked = padded[index]
        gate = bf16_blocks(picked, gate_w)
        up = bf16_blocks(picked, up_w)
        hidden = (jax.nn.silu(gate) * up).astype(jnp.bfloat16)
        produced = jnp.dot(hidden, down_w, preferred_element_type=jnp.float32).astype(jnp.bfloat16)
        total = total.at[index].add(weight[:, None] * produced.astype(jnp.float32))
        return total, None

    start = jnp.zeros((TOKENS + 1, D), jnp.float32)
    total, unused = lax.scan(one_expert, start, (table, weights, w_gate, w_up, w_down))
    return total[:TOKENS].astype(jnp.bfloat16)
```

```python
import jax
import jax.numpy as jnp
from jax import lax
from jax.sharding import Mesh, PartitionSpec as P

CAP = 4
NEAR = 4
LANES = 128
BF = jnp.bfloat16
F32 = jnp.float32
Z = ("zh", "zl")
XC = ("x", "c")


def dequantize(tokens_q, scale_exp):
    count, width = tokens_q.shape
    blocks = tokens_q.astype(F32).reshape(count, width // 128, 128)
    factor = jnp.exp2(scale_exp.astype(F32))[:, :, None]
    return (blocks * factor).reshape(count, width).astype(BF)


def shift(value, axis, step):
    size = lax.axis_size(axis)
    return lax.ppermute(value, axis, [(i, (i + step) % size) for i in range(size)])


def exchange(value, axis):
    return lax.all_to_all(value, axis, split_axis=0, concat_axis=0, tiled=True)


def ring_sum(chunk_of):
    size = lax.axis_size("y")
    right, left = size // 2, (size - 1) // 2
    to_right = chunk_of(right).astype(BF) if right else None
    to_left = chunk_of(-left).astype(BF) if left else None
    for step in range(right):
        to_right = shift(to_right, "y", 1)
        if step < left:
            to_left = shift(to_left, "y", -1)
        if step < right - 1:
            to_right = (chunk_of(right - 1 - step) + to_right.astype(F32)).astype(BF)
        if step < left - 1:
            to_left = (chunk_of(step + 1 - left) + to_left.astype(F32)).astype(BF)
    total = chunk_of(0)
    if right:
        total = total + to_right.astype(F32)
    if left:
        total = total + to_left.astype(F32)
    return total


def per_device(tokens_q, scale_exp, routes, route_scores, w_gate, w_up, w_down):
    n_x, n_c, n_y = lax.axis_size("x"), lax.axis_size("c"), lax.axis_size("y")
    n_z, n_zh = lax.axis_size(Z), lax.axis_size("zh")
    tok, feat = tokens_q.shape
    topk = routes.shape[1]
    hid = w_gate.shape[2]
    z = lax.axis_index(Z)
    y = lax.axis_index("y")
    peers = n_x * n_c
    slots = n_z * CAP

    rows = dequantize(tokens_q, scale_exp)
    mix = (2.5 * route_scores / jnp.sum(route_scores, axis=1, keepdims=True)).astype(BF)
    pad = jnp.zeros((tok, LANES - 2 * topk), BF)
    message = jnp.concatenate([rows, routes.astype(BF), mix, pad], axis=1)
    column = lax.all_gather(message, Z, axis=0, tiled=True)
    column_rows = column[:, :feat]
    column_routes = column[:, feat : feat + topk].astype(jnp.int32)
    column_mix = column[:, feat + topk : feat + 2 * topk].astype(F32)

    peer = jnp.arange(peers, dtype=jnp.int32)
    expert = (peer // n_c) * (n_z * n_c) + z * n_c + peer % n_c
    picked = column_routes[:, :, None] == expert[None, None, :]
    weight = jnp.sum(jnp.where(picked, column_mix[:, :, None], 0.0), axis=1)
    hit = jnp.any(picked, axis=1)
    named = hit.astype(jnp.int32).reshape(n_z, tok, peers)
    before = jnp.cumsum(named, axis=1, dtype=jnp.int32) - named
    block = jnp.arange(n_z, dtype=jnp.int32)[:, None, None]
    slot = jnp.where(named > 0, block * CAP + before, -1).reshape(n_z * tok, peers)
    slot_ids = jnp.arange(slots, dtype=jnp.int32)
    select = slot.T[:, None, :] == slot_ids[None, :, None]
    select_rows = select.astype(BF).reshape(peers * slots, n_z * tok)
    combine = jnp.where(select, weight.T[:, None, :], 0.0).astype(BF).reshape(peers * slots, n_z * tok)

    packed = jnp.dot(select_rows, column_rows, preferred_element_type=F32).astype(BF)
    arrived = exchange(packed.reshape(peers, slots, feat), XC).reshape(peers * slots, feat)

    gate_part = jnp.dot(arrived, w_gate[0], preferred_element_type=F32).astype(BF)
    up_part = jnp.dot(arrived, w_up[0], preferred_element_type=F32).astype(BF)
    share = peers * slots // n_y

    def chunk_of(k):
        start = ((y + k) % n_y) * share
        parts = [lax.dynamic_slice_in_dim(p, start, share, 0) for p in (gate_part, up_part)]
        return jnp.concatenate(parts, axis=1).astype(F32)

    total = ring_sum(chunk_of)
    hidden = (jax.nn.silu(total[:, :hid]) * total[:, hid:]).astype(BF)
    everywhere = jnp.broadcast_to(hidden[None], (n_y, share, hid))
    hidden_all = exchange(everywhere, "y").reshape(peers * slots, hid)

    produced = jnp.dot(hidden_all, w_down[0], preferred_element_type=F32).astype(BF)
    returned = exchange(produced.reshape(peers, slots, feat), XC).reshape(peers * slots, feat)

    partial = lax.dot_general(combine, returned, (((0,), (0,)), ((), ())), preferred_element_type=F32)
    partial = partial.reshape(n_zh, NEAR, tok, feat)
    residue = z % NEAR

    def near(k):
        return lax.dynamic_index_in_dim(partial, (residue + k) % NEAR, 1, keepdims=False)

    gathered = near(0)
    for k in (1, -1, 2):
        gathered = gathered + shift(near(k).astype(BF), Z, k).astype(F32)
    far = exchange(gathered.astype(BF), "zh")
    return jnp.sum(far.astype(F32), axis=0).astype(BF)


def solution(mesh):
    n_group, n_inner, n_cuts = mesh.devices.shape
    shape = (n_group, n_inner // 2 // NEAR, NEAR, 2, n_cuts)
    fine = Mesh(mesh.devices.reshape(shape), ("x", "zh", "zl", "c", "y"))
    owner = ("x", "zh", "zl", "c")
    in_specs = (
        P(owner, "y"),
        P(owner, "y"),
        P(owner, None),
        P(owner, None),
        P(owner, "y", None),
        P(owner, "y", None),
        P(owner, None, "y"),
    )
    return jax.shard_map(per_device, mesh=fine, in_specs=in_specs, out_specs=P(owner, "y"), check_vma=False)
```

```python
import jax
import jax.numpy as jnp
from jax import lax
from jax.experimental import pallas as pl
from jax.experimental.pallas import tpu as pltpu
from jax.sharding import Mesh, PartitionSpec as P

CAP = 4
LANES = 128
BF = jnp.bfloat16
F32 = jnp.float32
CHIPS = ("x", "z")


def message_kernel(tokens_ref, exp_ref, routes_ref, scores_ref, out_ref):
    tok, feat = tokens_ref.shape
    topk, blocks = routes_ref.shape[0], exp_ref.shape[0]
    factor = (1 << (exp_ref[...] + 16)).astype(F32) * (1.0 / 65536.0)
    scores = scores_ref[...]
    mix = 2.5 * scores / jnp.sum(scores, axis=0, keepdims=True)
    pad = jnp.zeros((LANES - 2 * topk - blocks, tok), F32)
    lines = jnp.concatenate([routes_ref[...].astype(F32), mix, factor, pad], axis=0).astype(BF)
    place = jax.lax.broadcasted_iota(jnp.int32, (LANES, LANES), 0)
    same = (place == jax.lax.broadcasted_iota(jnp.int32, (LANES, LANES), 1)).astype(BF)
    columns = lax.dot_general(lines, same, (((0,), (0,)), ((), ())), preferred_element_type=F32)
    for i in range(blocks):
        part = slice(i * LANES, (i + 1) * LANES)
        scale = columns[:, 2 * topk + i : 2 * topk + i + 1]
        out_ref[:, part] = (tokens_ref[:, part].astype(F32) * scale).astype(BF)
    out_ref[:, feat:] = columns.astype(BF)


def make_message(tokens_q, scale_exp, routes, route_scores):
    tok, feat = tokens_q.shape
    return pl.pallas_call(
        message_kernel,
        out_shape=jax.ShapeDtypeStruct((tok, feat + LANES), BF),
    )(tokens_q, scale_exp.T, routes.T, route_scores.T)


def along(value, step):
    size = lax.axis_size("y")
    return lax.ppermute(value, "y", [(i, (i + step) % size) for i in range(size)])


def exchange(value, axis):
    return lax.all_to_all(value, axis, split_axis=0, concat_axis=0, tiled=True)


def ring_sum(chunk_of, extra):
    size = lax.axis_size("y")
    right, left = size // 2, (size - 1) // 2
    width = chunk_of(0).shape[1]

    def join(k, arrived, block):
        part = chunk_of(k)
        if arrived is not None:
            part = part + arrived[:, :width].astype(F32)
        return jnp.concatenate([part.astype(BF), block], axis=1)

    total = extra.astype(F32)
    to_right = join(right, None, extra) if right else None
    to_left = join(-left, None, extra) if left else None
    for step in range(right):
        to_right = along(to_right, 1)
        if step < left:
            to_left = along(to_left, -1)
        total = total + to_right[:, width:].astype(F32)
        if step < left:
            total = total + to_left[:, width:].astype(F32)
        if step < right - 1:
            to_right = join(right - 1 - step, to_right, to_right[:, width:])
        if step < left - 1:
            to_left = join(step + 1 - left, to_left, to_left[:, width:])
    own = chunk_of(0)
    if right:
        own = own + to_right[:, :width].astype(F32)
    if left:
        own = own + to_left[:, :width].astype(F32)
    return own, total


def gated(gate, up):
    return (jax.nn.silu(gate) * up).astype(BF)


def per_device(tokens_q, scale_exp, routes, route_scores, w_gate, w_up, w_down):
    n_c, n_y, peers = lax.axis_size("c"), lax.axis_size("y"), lax.axis_size(CHIPS)
    tok, feat = tokens_q.shape
    topk = routes.shape[1]
    hid = w_gate.shape[2]
    tail_cols = LANES // (2 * n_y)
    core = lax.axis_index("c")
    y = lax.axis_index("y")
    slots = n_c * CAP
    total_rows = peers * slots

    message = make_message(tokens_q, scale_exp, routes, route_scores)
    pair = lax.all_gather(message, "c", axis=0, tiled=True)
    pair_routes = pair[:, feat : feat + topk].astype(jnp.int32)
    pair_mix = pair[:, feat + topk : feat + 2 * topk].astype(F32)

    expert = jnp.arange(peers, dtype=jnp.int32) * n_c + core
    picked = pair_routes[:, :, None] == expert[None, None, :]
    weight = jnp.sum(jnp.where(picked, pair_mix[:, :, None], 0.0), axis=1)
    named = jnp.any(picked, axis=1).astype(jnp.int32).reshape(n_c, tok, peers)
    before = jnp.cumsum(named, axis=1, dtype=jnp.int32) - named
    block = jnp.arange(n_c, dtype=jnp.int32)[:, None, None]
    slot = jnp.where(named > 0, block * CAP + before, -1).reshape(n_c * tok, peers)
    slot_ids = jnp.arange(slots, dtype=jnp.int32)
    select = slot.T[:, None, :] == slot_ids[None, :, None]
    select_rows = select.astype(BF).reshape(total_rows, n_c * tok)
    combine = jnp.where(select, weight.T[:, None, :], 0.0).astype(BF).reshape(total_rows, n_c * tok)

    packed = jnp.dot(select_rows, pair[:, :feat], preferred_element_type=F32).astype(BF)
    arrived = exchange(packed.reshape(peers, slots, feat), CHIPS).reshape(total_rows, feat)

    gate_part = jnp.dot(arrived, w_gate[0], preferred_element_type=F32).astype(BF)
    up_part = jnp.dot(arrived, w_up[0], preferred_element_type=F32).astype(BF)
    main = hid - tail_cols
    w_tail = jnp.concatenate([w_gate[0, :, main:], w_up[0, :, main:]], axis=1)
    tail_part = lax.dot_general(w_tail, arrived, (((0,), (1,)), ((), ())), preferred_element_type=F32).astype(BF)
    stacks = total_rows // LANES
    tail_part = tail_part.reshape(2 * tail_cols, stacks, LANES).transpose(1, 0, 2).reshape(stacks * 2 * tail_cols, LANES)
    share = total_rows // n_y

    def chunk_of(k):
        start = ((y + k) % n_y) * share
        parts = [lax.dynamic_slice_in_dim(p, start, share, 0) for p in (gate_part, up_part)]
        return jnp.concatenate(parts, axis=1).astype(F32)

    own, tail = ring_sum(chunk_of, tail_part)
    hidden = gated(own[:, :main], own[:, hid : hid + main])
    hidden_main = lax.all_gather(hidden, "y", axis=0, tiled=True)
    tail = tail.reshape(stacks, 2 * tail_cols, LANES).transpose(1, 0, 2).reshape(2 * tail_cols, total_rows)
    hidden_tail = gated(tail[:tail_cols], tail[tail_cols:])

    produced = jnp.dot(hidden_main, w_down[0, :main], preferred_element_type=F32)
    produced = produced + lax.dot_general(
        hidden_tail, w_down[0, main:], (((0,), (0,)), ((), ())), preferred_element_type=F32
    )
    returned = exchange(produced.astype(BF).reshape(peers, slots, feat), CHIPS).reshape(total_rows, feat)

    partial = lax.dot_general(combine, returned, (((0,), (0,)), ((), ())), preferred_element_type=F32)
    partial = partial.reshape(n_c, tok, feat)
    mine = lax.dynamic_index_in_dim(partial, core, 0, keepdims=False)
    theirs = lax.dynamic_index_in_dim(partial, 1 - core, 0, keepdims=False).astype(BF)
    return (mine + lax.ppermute(theirs, "c", [(0, 1), (1, 0)]).astype(F32)).astype(BF)


def solution(mesh):
    n_group, n_inner, n_cuts = mesh.devices.shape
    fine = Mesh(mesh.devices.reshape(n_group, n_inner // 2, 2, n_cuts), ("x", "z", "c", "y"))
    owner = ("x", "z", "c")
    in_specs = (
        P(owner, "y"),
        P(owner, "y"),
        P(owner, None),
        P(owner, None),
        P(owner, "y", None),
        P(owner, "y", None),
        P(owner, None, "y"),
    )
    return jax.shard_map(per_device, mesh=fine, in_specs=in_specs, out_specs=P(owner, "y"), check_vma=False)
```

```python
import jax
import jax.numpy as jnp
from jax import lax
from jax.experimental import pallas as pl
from jax.sharding import Mesh, PartitionSpec as P

CAP = 4
LANES = 128
BF = jnp.bfloat16
F32 = jnp.float32
CHIPS = ("x", "z")


def message_kernel(tokens_ref, exp_ref, routes_ref, scores_ref, out_ref):
    tok, feat = tokens_ref.shape
    topk, blocks = routes_ref.shape[0], exp_ref.shape[0]
    factor = (1 << (exp_ref[...] + 16)).astype(F32) * (1.0 / 65536.0)
    scores = scores_ref[...]
    mix = 2.5 * scores / jnp.sum(scores, axis=0, keepdims=True)
    pad = jnp.zeros((LANES - 2 * topk - blocks, tok), F32)
    lines = jnp.concatenate([routes_ref[...].astype(F32), mix, factor, pad], axis=0).astype(BF)
    place = jax.lax.broadcasted_iota(jnp.int32, (LANES, LANES), 0)
    same = (place == jax.lax.broadcasted_iota(jnp.int32, (LANES, LANES), 1)).astype(BF)
    columns = lax.dot_general(lines, same, (((0,), (0,)), ((), ())), preferred_element_type=F32)
    for i in range(blocks):
        part = slice(i * LANES, (i + 1) * LANES)
        scale = columns[:, 2 * topk + i : 2 * topk + i + 1]
        out_ref[:, part] = (tokens_ref[:, part].astype(F32) * scale).astype(BF)
    out_ref[:, feat:] = columns.astype(BF)


def make_message(tokens_q, scale_exp, routes, route_scores):
    tok, feat = tokens_q.shape
    return pl.pallas_call(
        message_kernel,
        out_shape=jax.ShapeDtypeStruct((tok, feat + LANES), BF),
    )(tokens_q, scale_exp.T, routes.T, route_scores.T)


def along(value, step):
    size = lax.axis_size("y")
    return lax.ppermute(value, "y", [(i, (i + step) % size) for i in range(size)])


def exchange(value, axis):
    return lax.all_to_all(value, axis, split_axis=0, concat_axis=0, tiled=True)


def ring_sum(chunk_of, extra):
    size = lax.axis_size("y")
    right, left = size // 2, (size - 1) // 2
    width = chunk_of(0).shape[1]

    def join(k, arrived, block):
        part = chunk_of(k)
        if arrived is not None:
            part = part + arrived[:, :width].astype(F32)
        return jnp.concatenate([part.astype(BF), block], axis=1)

    total = extra.astype(F32)
    to_right = join(right, None, extra) if right else None
    to_left = join(-left, None, extra) if left else None
    for step in range(right):
        to_right = along(to_right, 1)
        if step < left:
            to_left = along(to_left, -1)
        total = total + to_right[:, width:].astype(F32)
        if step < left:
            total = total + to_left[:, width:].astype(F32)
        if step < right - 1:
            to_right = join(right - 1 - step, to_right, to_right[:, width:])
        if step < left - 1:
            to_left = join(step + 1 - left, to_left, to_left[:, width:])
    own = chunk_of(0)
    if right:
        own = own + to_right[:, :width].astype(F32)
    if left:
        own = own + to_left[:, :width].astype(F32)
    return own, total


def gated(gate, up):
    return (jax.nn.silu(gate) * up).astype(BF)


def per_device(tokens_q, scale_exp, routes, route_scores, w_gate, w_up, w_down):
    n_c, n_y, peers = lax.axis_size("c"), lax.axis_size("y"), lax.axis_size(CHIPS)
    tok, feat = tokens_q.shape
    topk = routes.shape[1]
    hid = w_gate.shape[2]
    tail_cols = LANES // (2 * n_y)
    core = lax.axis_index("c")
    y = lax.axis_index("y")
    slots = n_c * CAP
    total_rows = peers * slots

    message = make_message(tokens_q, scale_exp, routes, route_scores)
    pair = lax.all_gather(message, "c", axis=0, tiled=True)
    pair_routes = pair[:, feat : feat + topk].astype(jnp.int32)
    pair_mix = pair[:, feat + topk : feat + 2 * topk].astype(F32)

    expert = jnp.arange(peers, dtype=jnp.int32) * n_c + core
    picked = pair_routes[:, :, None] == expert[None, None, :]
    weight = jnp.sum(jnp.where(picked, pair_mix[:, :, None], 0.0), axis=1)
    named = jnp.any(picked, axis=1).astype(jnp.int32).reshape(n_c, tok, peers)
    before = jnp.cumsum(named, axis=1, dtype=jnp.int32) - named
    block = jnp.arange(n_c, dtype=jnp.int32)[:, None, None]
    slot = jnp.where(named > 0, block * CAP + before, -1).reshape(n_c * tok, peers)
    slot_ids = jnp.arange(slots, dtype=jnp.int32)
    select = slot.T[:, None, :] == slot_ids[None, :, None]
    select_rows = select.astype(BF).reshape(total_rows, n_c * tok)
    combine = jnp.where(select, weight.T[:, None, :], 0.0).astype(BF).reshape(total_rows, n_c * tok)

    packed = jnp.dot(select_rows, pair[:, :feat], preferred_element_type=F32).astype(BF)
    arrived = exchange(packed.reshape(peers, slots, feat), CHIPS).reshape(total_rows, feat)

    gate_part = jnp.dot(arrived, w_gate[0], preferred_element_type=F32).astype(BF)
    up_part = jnp.dot(arrived, w_up[0], preferred_element_type=F32).astype(BF)
    main = hid - tail_cols
    w_tail = jnp.concatenate([w_gate[0, :, main:], w_up[0, :, main:]], axis=1)
    tail_part = lax.dot_general(w_tail, arrived, (((0,), (1,)), ((), ())), preferred_element_type=F32).astype(BF)
    stacks = total_rows // LANES
    tail_part = tail_part.reshape(2 * tail_cols, stacks, LANES).transpose(1, 0, 2).reshape(stacks * 2 * tail_cols, LANES)
    share = total_rows // n_y

    def chunk_of(k):
        start = ((y + k) % n_y) * share
        parts = [lax.dynamic_slice_in_dim(p, start, share, 0) for p in (gate_part, up_part)]
        return jnp.concatenate(parts, axis=1).astype(F32)

    own, tail = ring_sum(chunk_of, tail_part)
    hidden = gated(own[:, :main], own[:, hid : hid + main])
    hidden_main = lax.all_gather(hidden, "y", axis=0, tiled=True)
    tail = tail.reshape(stacks, 2 * tail_cols, LANES).transpose(1, 0, 2).reshape(2 * tail_cols, total_rows)
    hidden_tail = gated(tail[:tail_cols], tail[tail_cols:])

    hidden_all = jnp.concatenate([hidden_main, hidden_tail.T], axis=1)
    produced = jnp.dot(hidden_all, w_down[0], preferred_element_type=F32)
    returned = exchange(produced.astype(BF).reshape(peers, slots, feat), CHIPS).reshape(total_rows, feat)

    partial = lax.dot_general(combine, returned, (((0,), (0,)), ((), ())), preferred_element_type=F32)
    partial = partial.reshape(n_c, tok, feat)
    mine = lax.dynamic_index_in_dim(partial, core, 0, keepdims=False)
    theirs = lax.dynamic_index_in_dim(partial, 1 - core, 0, keepdims=False).astype(BF)
    crossed = lax.all_gather(theirs, "c", axis=0, tiled=False)
    crossed = lax.dynamic_index_in_dim(crossed, 1 - core, 0, keepdims=False)
    return (mine + crossed.astype(F32)).astype(BF)


def solution(mesh):
    n_group, n_inner, n_cuts = mesh.devices.shape
    fine = Mesh(mesh.devices.reshape(n_group, n_inner // 2, 2, n_cuts), ("x", "z", "c", "y"))
    owner = ("x", "z", "c")
    in_specs = (
        P(owner, "y"),
        P(owner, "y"),
        P(owner, None),
        P(owner, None),
        P(owner, "y", None),
        P(owner, "y", None),
        P(owner, None, "y"),
    )
    return jax.shard_map(per_device, mesh=fine, in_specs=in_specs, out_specs=P(owner, "y"), check_vma=False)
```

```python
import jax
import jax.numpy as jnp
from jax import lax
from jax.experimental import pallas as pl
from jax.sharding import Mesh, PartitionSpec as P

CAP = 4
LANES = 128
BF = jnp.bfloat16
F32 = jnp.float32
CHIPS = ("x", "z")


def message_kernel(tokens_ref, exp_ref, routes_ref, scores_ref, out_ref):
    tok, feat = tokens_ref.shape
    topk, blocks = routes_ref.shape[0], exp_ref.shape[0]
    factor = (1 << (exp_ref[...] + 16)).astype(F32) * (1.0 / 65536.0)
    scores = scores_ref[...]
    mix = 2.5 * scores / jnp.sum(scores, axis=0, keepdims=True)
    pad = jnp.zeros((LANES - 2 * topk - blocks, tok), F32)
    lines = jnp.concatenate([routes_ref[...].astype(F32), mix, factor, pad], axis=0).astype(BF)
    place = jax.lax.broadcasted_iota(jnp.int32, (LANES, LANES), 0)
    same = (place == jax.lax.broadcasted_iota(jnp.int32, (LANES, LANES), 1)).astype(BF)
    columns = lax.dot_general(lines, same, (((0,), (0,)), ((), ())), preferred_element_type=F32)
    for i in range(blocks):
        part = slice(i * LANES, (i + 1) * LANES)
        scale = columns[:, 2 * topk + i : 2 * topk + i + 1]
        out_ref[:, part] = (tokens_ref[:, part].astype(F32) * scale).astype(BF)
    out_ref[:, feat:] = columns.astype(BF)


def make_message(tokens_q, scale_exp, routes, route_scores):
    tok, feat = tokens_q.shape
    return pl.pallas_call(
        message_kernel,
        out_shape=jax.ShapeDtypeStruct((tok, feat + LANES), BF),
    )(tokens_q, scale_exp.T, routes.T, route_scores.T)


def along(value, step):
    size = lax.axis_size("y")
    return lax.ppermute(value, "y", [(i, (i + step) % size) for i in range(size)])


def exchange(value, axis):
    return lax.all_to_all(value, axis, split_axis=0, concat_axis=0, tiled=True)


def ring_sum(chunk_of, extra):
    size = lax.axis_size("y")
    steps = size // 2
    width = chunk_of(0).shape[1]
    half = width // 2

    def join(part, block):
        return jnp.concatenate([part.astype(BF), block], axis=1)

    total = extra.astype(F32)
    farthest = chunk_of(steps)
    to_right = join(farthest[:, :half], extra)
    to_left = join(farthest[:, half:], extra)
    for step in range(steps):
        to_right = along(to_right, 1)
        to_left = along(to_left, -1)
        right_block = to_right[:, -extra.shape[1] :]
        total = total + right_block.astype(F32)
        last = step == steps - 1
        if not last:
            left_block = to_left[:, -extra.shape[1] :]
            total = total + left_block.astype(F32)
        k = steps - 1 - step
        ahead, behind = chunk_of(k), chunk_of(-k)
        if step == 0:
            ahead = jnp.concatenate([ahead[:, :half] + to_right[:, :half].astype(F32), ahead[:, half:]], axis=1)
            behind = jnp.concatenate([behind[:, :half], behind[:, half:] + to_left[:, :half].astype(F32)], axis=1)
        elif not last:
            ahead = ahead + to_right[:, :width].astype(F32)
            behind = behind + to_left[:, :width].astype(F32)
        if not last:
            to_right = join(ahead, right_block)
            to_left = join(behind, left_block) if step < steps - 2 else behind.astype(BF)
    return chunk_of(0) + to_right[:, :width].astype(F32) + to_left[:, :width].astype(F32), total


def gated(gate, up):
    return (jax.nn.silu(gate) * up).astype(BF)


def per_device(tokens_q, scale_exp, routes, route_scores, w_gate, w_up, w_down):
    n_c, n_y, peers = lax.axis_size("c"), lax.axis_size("y"), lax.axis_size(CHIPS)
    tok, feat = tokens_q.shape
    topk = routes.shape[1]
    hid = w_gate.shape[2]
    tail_cols = LANES // (2 * n_y)
    core = lax.axis_index("c")
    y = lax.axis_index("y")
    slots = n_c * CAP
    total_rows = peers * slots

    message = make_message(tokens_q, scale_exp, routes, route_scores)
    pair = lax.all_gather(message, "c", axis=0, tiled=True)
    pair_routes = pair[:, feat : feat + topk].astype(jnp.int32)
    pair_mix = pair[:, feat + topk : feat + 2 * topk].astype(F32)

    expert = jnp.arange(peers, dtype=jnp.int32) * n_c + core
    picked = pair_routes[:, :, None] == expert[None, None, :]
    weight = jnp.sum(jnp.where(picked, pair_mix[:, :, None], 0.0), axis=1)
    named = jnp.any(picked, axis=1).astype(jnp.int32).reshape(n_c, tok, peers)
    before = jnp.cumsum(named, axis=1, dtype=jnp.int32) - named
    block = jnp.arange(n_c, dtype=jnp.int32)[:, None, None]
    slot = jnp.where(named > 0, block * CAP + before, -1).reshape(n_c * tok, peers)
    slot_ids = jnp.arange(slots, dtype=jnp.int32)
    select = slot.T[:, None, :] == slot_ids[None, :, None]
    select_rows = select.astype(BF).reshape(total_rows, n_c * tok)
    combine = jnp.where(select, weight.T[:, None, :], 0.0).astype(BF).reshape(total_rows, n_c * tok)

    packed = jnp.dot(select_rows, pair[:, :feat], preferred_element_type=F32).astype(BF)
    arrived = exchange(packed.reshape(peers, slots, feat), CHIPS).reshape(total_rows, feat)

    gate_part = jnp.dot(arrived, w_gate[0], preferred_element_type=F32).astype(BF)
    up_part = jnp.dot(arrived, w_up[0], preferred_element_type=F32).astype(BF)
    main = hid - tail_cols
    w_tail = jnp.concatenate([w_gate[0, :, main:], w_up[0, :, main:]], axis=1)
    tail_part = lax.dot_general(w_tail, arrived, (((0,), (1,)), ((), ())), preferred_element_type=F32).astype(BF)
    stacks = total_rows // LANES
    tail_part = tail_part.reshape(2 * tail_cols, stacks, LANES).transpose(1, 0, 2).reshape(stacks * 2 * tail_cols, LANES)
    share = total_rows // n_y

    def chunk_of(k):
        start = ((y + k) % n_y) * share
        parts = [lax.dynamic_slice_in_dim(p, start, share, 0) for p in (gate_part, up_part)]
        return jnp.concatenate(parts, axis=1).astype(F32)

    own, tail = ring_sum(chunk_of, tail_part)
    hidden = gated(own[:, :main], own[:, hid : hid + main])
    hidden_main = lax.all_gather(hidden, "y", axis=0, tiled=True)
    tail = tail.reshape(stacks, 2 * tail_cols, LANES).transpose(1, 0, 2).reshape(2 * tail_cols, total_rows)
    hidden_tail = gated(tail[:tail_cols], tail[tail_cols:])

    hidden_all = jnp.concatenate([hidden_main, hidden_tail.T], axis=1)
    produced = jnp.dot(hidden_all, w_down[0], preferred_element_type=F32)
    returned = exchange(produced.astype(BF).reshape(peers, slots, feat), CHIPS).reshape(total_rows, feat)

    partial = lax.dot_general(combine, returned, (((0,), (0,)), ((), ())), preferred_element_type=F32)
    partial = partial.reshape(n_c, tok, feat)
    mine = lax.dynamic_index_in_dim(partial, core, 0, keepdims=False)
    theirs = lax.dynamic_index_in_dim(partial, 1 - core, 0, keepdims=False).astype(BF)
    crossed = lax.all_gather(theirs, "c", axis=0, tiled=False)
    crossed = lax.dynamic_index_in_dim(crossed, 1 - core, 0, keepdims=False)
    return (mine + crossed.astype(F32)).astype(BF)


def solution(mesh):
    n_group, n_inner, n_cuts = mesh.devices.shape
    fine = Mesh(mesh.devices.reshape(n_group, n_inner // 2, 2, n_cuts), ("x", "z", "c", "y"))
    owner = ("x", "z", "c")
    in_specs = (
        P(owner, "y"),
        P(owner, "y"),
        P(owner, None),
        P(owner, None),
        P(owner, "y", None),
        P(owner, "y", None),
        P(owner, None, "y"),
    )
    return jax.shard_map(per_device, mesh=fine, in_specs=in_specs, out_specs=P(owner, "y"), check_vma=False)
```

```python
import functools

import jax
import jax.numpy as jnp
from jax import lax
from jax.experimental import pallas as pl
from jax.sharding import Mesh, PartitionSpec as P

CAP = 4
LANES = 128
BF = jnp.bfloat16
F32 = jnp.float32
CHIPS = ("x", "z")


def message_kernel(n_experts, tokens_ref, exp_ref, routes_ref, scores_ref, out_ref):
    tok, feat = tokens_ref.shape
    topk, blocks = routes_ref.shape[0], exp_ref.shape[0]
    factor = (1 << (exp_ref[...] + 16)).astype(F32) * (1.0 / 65536.0)
    scores = scores_ref[...]
    mix = 2.5 * scores / jnp.sum(scores, axis=0, keepdims=True)
    pad = jnp.zeros((LANES - 2 * topk - blocks, tok), F32)
    lines = jnp.concatenate([routes_ref[...].astype(F32), mix, factor, pad], axis=0).astype(BF)
    place = jax.lax.broadcasted_iota(jnp.int32, (LANES, LANES), 0)
    same = (place == jax.lax.broadcasted_iota(jnp.int32, (LANES, LANES), 1)).astype(BF)
    columns = lax.dot_general(lines, same, (((0,), (0,)), ((), ())), preferred_element_type=F32)
    for i in range(blocks):
        part = slice(i * LANES, (i + 1) * LANES)
        scale = columns[:, 2 * topk + i : 2 * topk + i + 1]
        out_ref[:, part] = (tokens_ref[:, part].astype(F32) * scale).astype(BF)
    lane = lax.broadcasted_iota(jnp.int32, (tok, 2 * LANES), 1)
    peer, core = lane % LANES, lane // LANES
    expert = jnp.where(peer < n_experts // 2, peer * 2 + core, -1).astype(F32)
    named = jnp.zeros((tok, 2 * LANES), F32)
    weight = jnp.zeros((tok, 2 * LANES), F32)
    for k in range(topk):
        hit = columns[:, k : k + 1] == expert
        named = jnp.where(hit, 1.0, named)
        weight = jnp.where(hit, columns[:, topk + k : topk + k + 1], weight)
    order = lax.broadcasted_iota(jnp.int32, (tok, tok), 0) > lax.broadcasted_iota(jnp.int32, (tok, tok), 1)
    before = jnp.dot(order.astype(BF), named.astype(BF), preferred_element_type=F32)
    slot = jnp.where(named > 0.0, before, -1.0)
    for c in range(2):
        part = slice(c * LANES, (c + 1) * LANES)
        at = feat + 2 * c * LANES
        out_ref[:, at : at + LANES] = slot[:, part].astype(BF)
        out_ref[:, at + LANES : at + 2 * LANES] = weight[:, part].astype(BF)


def make_message(tokens_q, scale_exp, routes, route_scores, n_experts):
    tok, feat = tokens_q.shape
    return pl.pallas_call(
        functools.partial(message_kernel, n_experts),
        out_shape=jax.ShapeDtypeStruct((tok, feat + 4 * LANES), BF),
    )(tokens_q, scale_exp.T, routes.T, route_scores.T)


def along(value, step):
    size = lax.axis_size("y")
    return lax.ppermute(value, "y", [(i, (i + step) % size) for i in range(size)])


def exchange(value, axis):
    return lax.all_to_all(value, axis, split_axis=0, concat_axis=0, tiled=True)


def ring_sum(chunk_of, extra):
    size = lax.axis_size("y")
    steps = size // 2
    width = chunk_of(0).shape[1]
    half = width // 2

    def join(part, block):
        return jnp.concatenate([part.astype(BF), block], axis=1)

    total = extra.astype(F32)
    farthest = chunk_of(steps)
    to_right = join(farthest[:, :half], extra)
    to_left = join(farthest[:, half:], extra)
    for step in range(steps):
        to_right = along(to_right, 1)
        to_left = along(to_left, -1)
        right_block = to_right[:, -extra.shape[1] :]
        total = total + right_block.astype(F32)
        last = step == steps - 1
        if not last:
            left_block = to_left[:, -extra.shape[1] :]
            total = total + left_block.astype(F32)
        k = steps - 1 - step
        ahead, behind = chunk_of(k), chunk_of(-k)
        if step == 0:
            ahead = jnp.concatenate([ahead[:, :half] + to_right[:, :half].astype(F32), ahead[:, half:]], axis=1)
            behind = jnp.concatenate([behind[:, :half], behind[:, half:] + to_left[:, :half].astype(F32)], axis=1)
        elif not last:
            ahead = ahead + to_right[:, :width].astype(F32)
            behind = behind + to_left[:, :width].astype(F32)
        if not last:
            to_right = join(ahead, right_block)
            to_left = join(behind, left_block) if step < steps - 2 else behind.astype(BF)
    return chunk_of(0) + to_right[:, :width].astype(F32) + to_left[:, :width].astype(F32), total


def gated(gate, up):
    return (jax.nn.silu(gate) * up).astype(BF)


def per_device(tokens_q, scale_exp, routes, route_scores, w_gate, w_up, w_down):
    n_c, n_y, peers = lax.axis_size("c"), lax.axis_size("y"), lax.axis_size(CHIPS)
    tok, feat = tokens_q.shape
    hid = w_gate.shape[2]
    tail_cols = LANES // (2 * n_y)
    core = lax.axis_index("c")
    y = lax.axis_index("y")
    slots = n_c * CAP
    total_rows = peers * slots

    message = make_message(tokens_q, scale_exp, routes, route_scores, peers * n_c)
    pair = lax.all_gather(message, "c", axis=0, tiled=True)
    mine = lax.dynamic_slice_in_dim(pair, feat + core * 2 * LANES, 2 * LANES, 1)
    weight = mine[:, LANES : LANES + peers].astype(F32)
    block = jnp.arange(n_c * tok, dtype=jnp.int32)[:, None] // tok
    slot = mine[:, :peers].astype(jnp.int32)
    slot = jnp.where(slot >= 0, block * CAP + slot, -1)
    slot_ids = jnp.arange(slots, dtype=jnp.int32)
    select = slot.T[:, None, :] == slot_ids[None, :, None]
    select_rows = select.astype(BF).reshape(total_rows, n_c * tok)
    combine = jnp.where(select, weight.T[:, None, :], 0.0).astype(BF).reshape(total_rows, n_c * tok)

    packed = jnp.dot(select_rows, pair[:, :feat], preferred_element_type=F32).astype(BF)
    arrived = exchange(packed.reshape(peers, slots, feat), CHIPS).reshape(total_rows, feat)

    gate_part = jnp.dot(arrived, w_gate[0], preferred_element_type=F32).astype(BF)
    up_part = jnp.dot(arrived, w_up[0], preferred_element_type=F32).astype(BF)
    main = hid - tail_cols
    w_tail = jnp.concatenate([w_gate[0, :, main:], w_up[0, :, main:]], axis=1)
    tail_part = lax.dot_general(w_tail, arrived, (((0,), (1,)), ((), ())), preferred_element_type=F32).astype(BF)
    stacks = total_rows // LANES
    tail_part = tail_part.reshape(2 * tail_cols, stacks, LANES).transpose(1, 0, 2).reshape(stacks * 2 * tail_cols, LANES)
    share = total_rows // n_y

    def chunk_of(k):
        start = ((y + k) % n_y) * share
        parts = [lax.dynamic_slice_in_dim(p, start, share, 0) for p in (gate_part, up_part)]
        return jnp.concatenate(parts, axis=1).astype(F32)

    own, tail = ring_sum(chunk_of, tail_part)
    hidden = gated(own[:, :main], own[:, hid : hid + main])
    hidden_main = lax.all_gather(hidden, "y", axis=0, tiled=True)
    tail = tail.reshape(stacks, 2 * tail_cols, LANES).transpose(1, 0, 2).reshape(2 * tail_cols, total_rows)
    hidden_tail = gated(tail[:tail_cols], tail[tail_cols:])

    hidden_all = jnp.concatenate([hidden_main, hidden_tail.T], axis=1)
    produced = jnp.dot(hidden_all, w_down[0], preferred_element_type=F32)
    returned = exchange(produced.astype(BF).reshape(peers, slots, feat), CHIPS).reshape(total_rows, feat)

    partial = lax.dot_general(combine, returned, (((0,), (0,)), ((), ())), preferred_element_type=F32)
    partial = partial.reshape(n_c, tok, feat)
    mine = lax.dynamic_index_in_dim(partial, core, 0, keepdims=False)
    theirs = lax.dynamic_index_in_dim(partial, 1 - core, 0, keepdims=False).astype(BF)
    crossed = lax.all_gather(theirs, "c", axis=0, tiled=False)
    crossed = lax.dynamic_index_in_dim(crossed, 1 - core, 0, keepdims=False)
    return (mine + crossed.astype(F32)).astype(BF)


def solution(mesh):
    n_group, n_inner, n_cuts = mesh.devices.shape
    fine = Mesh(mesh.devices.reshape(n_group, n_inner // 2, 2, n_cuts), ("x", "z", "c", "y"))
    owner = ("x", "z", "c")
    in_specs = (
        P(owner, "y"),
        P(owner, "y"),
        P(owner, None),
        P(owner, None),
        P(owner, "y", None),
        P(owner, "y", None),
        P(owner, None, "y"),
    )
    return jax.shard_map(per_device, mesh=fine, in_specs=in_specs, out_specs=P(owner, "y"), check_vma=False)
```
